256 devices in a mesh: section: 2 (over core), seq: 128 (over z, y, x).
Axes of the slice: x: 4, y: 4, z: 8, core: 2. Of those that a mesh axis runs over, the one named last changes fastest.
Arguments:
- queries: bfloat16 [32768, 4096], P('seq', 'section'), may hold values from -50 to 50
- key_rows: bfloat16 [32768, 4096], P('seq', 'section'), may hold values from -6 to 6
- value_rows: bfloat16 [32768, 4096], P('seq', 'section'), may hold values from -6 to 6
- block_pattern: int32 [256, 8], P('seq'), may hold values from 0 to 1, as said below
- out_weight: bfloat16 [4096, 4096], P('section'), may hold values from -0.09375 to 0.09375
- hidden: bfloat16 [32768, 4096], P('seq', 'section'), may hold values from -3 to 3
- norm_gain: float32 [4096], P('section'), may hold values from 0.5 to 1.5
Outputs:
- stream_out: bfloat16 [32768, 4096], P('seq', 'section')
- normed: bfloat16 [32768, 4096], P('seq', 'section')
The draws below stay inside these ranges and needn't reach their ends.
Inputs may be any that keep to these rules, and one draw needn't show every extreme that they name: `block_pattern`: column 0 is 1 in every row: every query block attends its own block.
All inputs are finite; a program needn't handle non-finite values.
Results may differ from the reference program's by a relative error of at most 0.008.
Values may be sent and summed in bfloat16 or wider, within the bound.
No kernel may reach another device: no remote copies, remote signals or barrier semaphores. Data moves between devices by JAX's collectives and lax.ppermute only.
A program may use at most 128 MiB of HBM per device.

```python
import math
import jax
import jax.numpy as jnp
from jax import lax

D = 4096
HEADS = 32
HEAD_DIM = 128
BLOCK = 128
WINDOW_BLOCKS = 8
TOKENS = 32768
NBLK = 256
N_SECTION = 2


def joint_draw(key):
    full_shape = (TOKENS, D)
    query_key = jax.random.fold_in(key, 101)
    keys_key = jax.random.fold_in(key, 202)
    query_draw = jnp.clip(2.0 * jax.random.normal(query_key, full_shape, jnp.float32), -12.0, 12.0)
    key_draw = jnp.clip(jax.random.normal(keys_key, full_shape, jnp.float32), -6.0, 6.0)
    return (query_draw, key_draw)


def draw_queries(key, part):
    query_draw, key_draw = joint_draw(key)
    return query_draw.astype(jnp.bfloat16)


def draw_key_rows(key, part):
    query_draw, key_draw = joint_draw(key)
    return key_draw.astype(jnp.bfloat16)


def draw_block_pattern(key, part):
    picked = jax.random.randint(jax.random.fold_in(key, 303), (NBLK, WINDOW_BLOCKS), 0, 2, jnp.int32)
    column = jnp.arange(WINDOW_BLOCKS, dtype=jnp.int32)[None, :]
    return jnp.where(column == 0, 1, picked).astype(jnp.int32)


def draw_hidden(key, part):
    column_scale = 0.5 + jnp.arange(D, dtype=jnp.float32) / D
    base_key = jax.random.fold_in(key, 404)
    noise = jnp.clip(jax.random.normal(base_key, (TOKENS, D), jnp.float32), -6.0, 6.0)
    values = 0.3 * noise * column_scale[None, :]
    return values.astype(jnp.bfloat16)


def block_levels(rng, extent, shards, low, top_value):
    def one(dim, blocks):
        draws = jax.random.uniform(jax.random.fold_in(jax.random.fold_in(rng, 6), dim), (blocks,), jnp.float32, low / len(shards), top_value / len(shards))
        return jnp.repeat(jnp.exp(draws), extent[dim] // blocks).reshape((-1,) + (1,) * (len(extent) - dim - 1))

    level = one(*shards[0])
    for cut in shards[1:]:
        level = level * one(*cut)
    return level


def gaussian(key, dims, deviation, bound, pieces=(), kind=jnp.bfloat16):
    values = deviation * jax.random.normal(key, dims, jnp.float32)
    if pieces:
        values = values * block_levels(key, dims, pieces, -0.22, 0.18)
    return jnp.clip(values, -bound, bound).astype(kind)


def setup_inputs(seed: int = 0) -> dict:
    keys = jax.random.split(jax.random.key(seed), 8)
    return {
        "queries": draw_queries(jax.random.fold_in(keys[7], 71), 0),
        "key_rows": draw_key_rows(jax.random.fold_in(keys[7], 71), 0),
        "value_rows": gaussian(keys[2], (TOKENS, D), 1.0, 6.0, ((0, 128), (1, 2))),
        "block_pattern": draw_block_pattern(jax.random.fold_in(keys[7], 71), 0),
        "out_weight": gaussian(keys[4], (D, D), D ** -0.5, 0.09375, ((0, 2),)),
        "hidden": draw_hidden(jax.random.fold_in(keys[7], 71), 0),
        "norm_gain": jnp.clip(1.0 + 0.1 * jax.random.normal(keys[6], (D,), jnp.float32), 0.5, 1.5),
    }


def window_attention(queries, key_rows, value_rows, block_pattern):
    token_count = queries.shape[0]
    block_count = token_count // BLOCK
    front_rows = (WINDOW_BLOCKS - 1) * BLOCK
    padded_keys = jnp.concatenate([jnp.zeros((front_rows, D), key_rows.dtype), key_rows], 0)
    padded_values = jnp.concatenate([jnp.zeros((front_rows, D), value_rows.dtype), value_rows], 0)
    window_span = WINDOW_BLOCKS * BLOCK
    offsets = (WINDOW_BLOCKS - 1 - jnp.arange(window_span, dtype=jnp.int32) // BLOCK).astype(jnp.int32)
    key_place = jnp.arange(window_span, dtype=jnp.int32) % BLOCK
    query_place = jnp.arange(BLOCK, dtype=jnp.int32)
    scaling = 1.0 / math.sqrt(HEAD_DIM)

    def one_block(block_index):
        begin_row = (block_index * BLOCK).astype(jnp.int32)
        query_block = lax.dynamic_slice_in_dim(queries, begin_row, BLOCK, 0).astype(jnp.float32).reshape(BLOCK, HEADS, HEAD_DIM)
        key_block = lax.dynamic_slice_in_dim(padded_keys, begin_row, window_span, 0).astype(jnp.float32).reshape(window_span, HEADS, HEAD_DIM)
        value_block = lax.dynamic_slice_in_dim(padded_values, begin_row, window_span, 0).astype(jnp.float32).reshape(window_span, HEADS, HEAD_DIM)
        pattern_row = lax.dynamic_index_in_dim(block_pattern, block_index, 0, keepdims=False)
        allowed = (pattern_row[offsets] == 1) & (block_index - offsets >= 0)
        causal = (offsets[None, :] > 0) | (key_place[None, :] <= query_place[:, None])
        visible = allowed[None, :] & causal
        scores = jnp.einsum('qhd,khd->hqk', query_block, key_block) * scaling
        scores = jnp.where(visible[None], scores, -jnp.inf)
        largest = lax.optimization_barrier(jnp.max(scores, axis=2, keepdims=True))
        exponent = jnp.exp(scores - largest)
        weights = (exponent / lax.optimization_barrier(jnp.sum(exponent, axis=2, keepdims=True))).astype(jnp.bfloat16)
        mixture = jnp.einsum('hqk,khd->qhd', weights.astype(jnp.float32), value_block)
        return mixture.reshape(BLOCK, D).astype(jnp.bfloat16)
    result = lax.map(one_block, jnp.arange(block_count, dtype=jnp.int32))
    return result.reshape(token_count, D)

def reference(queries, key_rows, value_rows, block_pattern, out_weight, hidden, norm_gain):
    attended = window_attention(queries, key_rows, value_rows, block_pattern)
    group_width = D // N_SECTION
    projected = jnp.zeros((TOKENS, D), jnp.float32)
    for group_index in range(N_SECTION):
        low = group_index * group_width
        group_part = jnp.dot(attended[:, low:low + group_width], out_weight[low:low + group_width], preferred_element_type=jnp.float32).astype(jnp.bfloat16)
        projected = projected + lax.optimization_barrier(group_part).astype(jnp.float32)
    stream = hidden.astype(jnp.float32) + projected
    mean_square = lax.optimization_barrier(jnp.mean(stream * stream, axis=1, keepdims=True))
    normed = stream * lax.rsqrt(mean_square + 1e-06) * norm_gain[None, :]
    return (stream.astype(jnp.bfloat16), normed.astype(jnp.bfloat16))
```

```python
import math

import jax
import jax.numpy as jnp
from jax import lax
from jax.experimental import pallas as pl
from jax.experimental.pallas import tpu as pltpu
from jax.sharding import PartitionSpec as P

D = 4096
HALF = 2048
HEAD_DIM = 128
BLOCK = 128
WINDOW = 8
ROWS = 256
RING = 4
SLOTS = 1
WIDTH = 512 // SLOTS
HIDE = -3e38
VMEM = 12 * 1024 * 1024


def ring_shift(array, d):
    route = [(i, (i // RING) * RING + (i + d) % RING) for i in range(128)]
    return lax.ppermute(array, "seq", route)


def next_row(array):
    return lax.ppermute(array, "seq", [(i, i + RING) for i in range(128 - RING)])


def other_core(array):
    return lax.ppermute(array, "section", [(0, 1), (1, 0)])


def after(array, *others):
    return lax.optimization_barrier((array,) + others)[0]


def attend_kernel(order, x_ref, *refs):
    own = refs[0:4]
    halo = refs[4:8]
    count = len(order)
    qs = refs[8 : 8 + count]
    outs = refs[8 + count : 8 + 2 * count]
    kbuf, vbuf = refs[8 + 2 * count :]
    x = x_ref[0]
    for d in range(RING):
        j = (x + RING - d) & 3
        far = pl.multiple_of(j * ROWS, ROWS)
        near = pl.multiple_of(j * ROWS + RING * ROWS, ROWS)
        kbuf[pl.ds(far, ROWS), :] = halo[d][0:ROWS, :]
        vbuf[pl.ds(far, ROWS), :] = halo[d][ROWS : 2 * ROWS, :]
        kbuf[pl.ds(near, ROWS), :] = own[d][0:ROWS, :]
        vbuf[pl.ds(near, ROWS), :] = own[d][ROWS : 2 * ROWS, :]
    row = lax.broadcasted_iota(jnp.int32, (BLOCK, BLOCK), 0)
    col = lax.broadcasted_iota(jnp.int32, (BLOCK, BLOCK), 1)
    causal = col <= row
    factor = math.log2(math.e) / math.sqrt(HEAD_DIM)
    for index, d in enumerate(order):
        j = (x + RING - d) & 3
        for r in range(2):
            start = pl.multiple_of((2 * j + r + 1) * BLOCK, BLOCK)
            span = pl.ds(start, WINDOW * BLOCK)
            q = qs[index][r * BLOCK : (r + 1) * BLOCK, :]
            hide = qs[index][ROWS : ROWS + 16, :].astype(jnp.float32)
            s = lax.dot_general(
                q, kbuf[span, :], (((1,), (1,)), ((), ())), preferred_element_type=jnp.float32
            )
            parts = []
            for i in range(WINDOW - 1):
                line = hide[r * 8 + i : r * 8 + i + 1, :]
                parts.append(s[:, i * BLOCK : (i + 1) * BLOCK] + line)
            parts.append(jnp.where(causal, s[:, (WINDOW - 1) * BLOCK :], HIDE))
            top = parts[0]
            for part in parts[1:]:
                top = jnp.maximum(top, part)
            top = jnp.max(top, axis=1, keepdims=True)
            parts = [jnp.exp2((part - top) * factor) for part in parts]
            total = parts[0]
            for part in parts[1:]:
                total = total + part
            total = jnp.sum(total, axis=1, keepdims=True)
            p = jnp.concatenate([part.astype(jnp.bfloat16) for part in parts], axis=1)
            o = jnp.dot(p, vbuf[span, :], preferred_element_type=jnp.float32)
            outs[index][r * BLOCK : (r + 1) * BLOCK, :] = (o / total).astype(jnp.bfloat16)


def attend(x, own, halo, qs, order):
    count = len(order)
    piece = pl.BlockSpec((2 * ROWS, HEAD_DIM), lambda h, x: (0, h))
    query = pl.BlockSpec((ROWS + 16, HEAD_DIM), lambda h, x: (0, h))
    result = pl.BlockSpec((ROWS, HEAD_DIM), lambda h, x: (0, h))
    return pl.pallas_call(
        lambda *refs: attend_kernel(order, *refs),
        out_shape=[jax.ShapeDtypeStruct((ROWS, WIDTH), jnp.bfloat16)] * count,
        grid_spec=pltpu.PrefetchScalarGridSpec(
            num_scalar_prefetch=1,
            grid=(WIDTH // HEAD_DIM,),
            in_specs=[piece] * 8 + [query] * count,
            out_specs=[result] * count,
            scratch_shapes=[pltpu.VMEM((2 * RING * ROWS, HEAD_DIM), jnp.bfloat16)] * 2,
        ),
        compiler_params=pltpu.CompilerParams(vmem_limit_bytes=VMEM),
        cost_estimate=pl.CostEstimate(
            flops=count * 1100000000 // 2 // SLOTS,
            bytes_accessed=5000000 // SLOTS,
            transcendentals=count * 1000000 // SLOTS,
        ),
        name="attend",
    )(x, *own, *halo, *qs)


TILE = 512


def project_kernel(x_ref, *refs):
    count = (len(refs) - 1) // 2
    total = None
    for o, w in zip(refs[:count], refs[count : 2 * count]):
        term = jnp.dot(o[...], w[...], preferred_element_type=jnp.float32)
        total = term if total is None else total + term
    refs[-1][...] = total.astype(jnp.bfloat16)


def project(x, pieces, weight):
    keys = list(pieces)
    values = [pieces[key] for key in keys]

    def weight_block(d, s):
        return pl.BlockSpec((WIDTH, TILE), lambda n, x: (((x[0] + d) & 3) * SLOTS + s, n))

    return pl.pallas_call(
        project_kernel,
        out_shape=jax.ShapeDtypeStruct((ROWS, D), jnp.bfloat16),
        grid_spec=pltpu.PrefetchScalarGridSpec(
            num_scalar_prefetch=1,
            grid=(D // TILE,),
            in_specs=[pl.BlockSpec((ROWS, WIDTH), lambda n, x: (0, 0)) for _ in keys]
            + [weight_block(d, s) for d, s in keys],
            out_specs=pl.BlockSpec((ROWS, TILE), lambda n, x: (0, n)),
        ),
        compiler_params=pltpu.CompilerParams(vmem_limit_bytes=VMEM),
        cost_estimate=pl.CostEstimate(
            flops=2 * ROWS * HALF * D, bytes_accessed=20000000, transcendentals=0
        ),
        name="project",
    )(x, *values, *([weight] * len(keys)))


STRIP = 64


def finish_kernel(s_ref, near, far, hidden_own, hidden_other, gain, stream_ref, normed_ref):
    side = pl.multiple_of(s_ref[0] * HALF, HALF)
    away = pl.multiple_of((1 - s_ref[0]) * HALF, HALF)

    def stream_of(columns, hidden):
        total = near[:, columns].astype(jnp.float32) + far[:, columns].astype(jnp.float32)
        return hidden[...].astype(jnp.float32) + total

    mine = stream_of(pl.ds(side, HALF), hidden_own)
    rest = stream_of(pl.ds(away, HALF), hidden_other)
    squares = jnp.sum(mine * mine + rest * rest, axis=1, keepdims=True)
    factor = lax.rsqrt(squares / D + 1e-06)
    stream_ref[...] = mine.astype(jnp.bfloat16)
    normed_ref[...] = (mine * factor * gain[...]).astype(jnp.bfloat16)


def finish(section, near, far, hidden_own, hidden_other, gain):
    whole = pl.BlockSpec((STRIP, D), lambda i, s: (i, 0))
    half = pl.BlockSpec((STRIP, HALF), lambda i, s: (i, 0))
    return pl.pallas_call(
        finish_kernel,
        out_shape=[jax.ShapeDtypeStruct((ROWS, HALF), jnp.bfloat16)] * 2,
        grid_spec=pltpu.PrefetchScalarGridSpec(
            num_scalar_prefetch=1,
            grid=(ROWS // STRIP,),
            in_specs=[whole, whole, half, half, pl.BlockSpec((1, HALF), lambda i, s: (0, 0))],
            out_specs=[half, half],
        ),
        compiler_params=pltpu.CompilerParams(vmem_limit_bytes=VMEM),
        cost_estimate=pl.CostEstimate(flops=10000000, bytes_accessed=8000000, transcendentals=256),
        name="finish",
    )(section, near, far, hidden_own, hidden_other, gain.reshape(1, HALF))


def hide_rows(block_pattern, shard):
    back = WINDOW - 1 - jnp.arange(WINDOW, dtype=jnp.int32)[None, :]
    query_block = shard * 2 + jnp.arange(2, dtype=jnp.int32)[:, None]
    allowed = (block_pattern[:, ::-1] == 1) & (query_block - back >= 0)
    flags = jnp.where(allowed, 0.0, HIDE).astype(jnp.bfloat16).reshape(16, 1)
    return jnp.broadcast_to(flags, (16, WIDTH))


def shards(queries, key_rows, value_rows, block_pattern, out_weight, hidden, norm_gain):
    shard = lax.axis_index("seq")
    section = lax.axis_index("section").astype(jnp.int32)
    x = (shard % RING).astype(jnp.int32)
    hide = hide_rows(block_pattern, shard)

    def cut(array, d, s):
        begin = ((x + d) % RING) * 512 + s * WIDTH
        return lax.dynamic_slice(array, (jnp.int32(0), begin), (ROWS, WIDTH))

    def pack_kv(d, s):
        return jnp.concatenate([cut(key_rows, d, s), cut(value_rows, d, s)], 0)

    def pack_q(d, s):
        return jnp.concatenate([cut(queries, d, s), hide], 0)

    hidden_other = other_core(hidden)
    pieces = {}
    for s in range(SLOTS):
        own, halo, qs = [None] * 4, [None] * 4, [None] * 4
        own[0] = pack_kv(0, s)
        for d in (1, 3):
            own[d] = ring_shift(pack_kv(d, s), d)
        halo[0] = next_row(own[0])
        own[2] = ring_shift(after(pack_kv(2, s), own[1], own[3]), 2)
        for d in (1, 3):
            qs[d] = ring_shift(after(pack_q(d, s), own[1], own[3]), d)
        for d in (1, 3, 2):
            halo[d] = next_row(own[d])
        qs[2] = ring_shift(after(pack_q(2, s), own[2], hidden_other), 2)
        qs[0] = pack_q(0, s)
        xs = x.reshape(1)
        for order in ((2, 1), (3, 0)):
            outs = attend(xs, own, halo, [qs[d] for d in order], order)
            for d, out in zip(order, outs):
                pieces[d, s] = ring_shift(out, -d) if d else out
    near = project(x.reshape(1), pieces, out_weight)
    far = other_core(near)
    return tuple(
        finish(section.reshape(1), near, far, hidden, hidden_other, norm_gain)
    )


def solution(mesh):
    placed = (
        P("seq", "section"),
        P("seq", "section"),
        P("seq", "section"),
        P("seq", None),
        P("section", None),
        P("seq", "section"),
        P("section"),
    )
    return jax.shard_map(
        shards,
        mesh=mesh,
        in_specs=placed,
        out_specs=(P("seq", "section"), P("seq", "section")),
        check_vma=False,
    )
```

```python
import math

import jax
import jax.numpy as jnp
from jax import lax
from jax.experimental import pallas as pl
from jax.experimental.pallas import tpu as pltpu
from jax.sharding import PartitionSpec as P

D = 4096
HALF = 2048
HEAD_DIM = 128
BLOCK = 128
WINDOW = 8
ROWS = 256
RING = 4
WIDTH = 512
HIDE = -3e38
VMEM = 16 * 1024 * 1024


def ring_shift(array, d):
    route = [(i, (i // RING) * RING + (i + d) % RING) for i in range(128)]
    return lax.ppermute(array, "seq", route)


def next_row(array):
    return lax.ppermute(array, "seq", [(i, (i + RING) % 128) for i in range(128)])


def other_core(array):
    return lax.ppermute(array, "section", [(0, 1), (1, 0)])


def after(array, *others):
    return lax.optimization_barrier((array,) + others)[0]


FACTOR = math.log2(math.e) / math.sqrt(HEAD_DIM)


def dot_keys(q, keys):
    return lax.dot_general(q, keys, (((1,), (1,)), ((), ())), preferred_element_type=jnp.float32)


def fold(step, parts):
    result = parts[0]
    for part in parts[1:]:
        result = step(result, part)
    return result


NEAR_UNROLL = 4
FAR_UNROLL = 4


def heads_in_turn(head, unroll):
    def step(i, carry):
        for k in range(unroll):
            head(i * unroll + k)
        return carry

    if unroll == WIDTH // HEAD_DIM:
        step(0, 0)
    else:
        lax.fori_loop(0, WIDTH // HEAD_DIM // unroll, step, 0)


def head_columns(h):
    if isinstance(h, int):
        return slice(h * HEAD_DIM, (h + 1) * HEAD_DIM)
    return pl.ds(pl.multiple_of(h * HEAD_DIM, HEAD_DIM), HEAD_DIM)


def head_pair(h):
    if isinstance(h, int):
        return slice(h * 2 * HEAD_DIM, (h + 1) * 2 * HEAD_DIM)
    return pl.ds(pl.multiple_of(h * 2 * HEAD_DIM, 2 * HEAD_DIM), 2 * HEAD_DIM)


def spread_values(vbuf, at, values):
    ones = jnp.ones((ROWS, HEAD_DIM), jnp.bfloat16)
    for h in range(WIDTH // HEAD_DIM):
        here = slice(h * HEAD_DIM, (h + 1) * HEAD_DIM)
        vbuf[at, head_pair(h)] = jnp.concatenate([values[:, here], ones], axis=1)


def place_halo(x, d, piece, base, kfar, vfar):
    at = pl.ds(pl.multiple_of(((x + RING - d) & 3) * ROWS, ROWS), ROWS)
    kfar[at, :] = piece[base : base + ROWS, :]
    spread_values(vfar, at, piece[base + ROWS : base + 2 * ROWS, :])


def near_kernel(x_ref, *refs):
    own, qs, halo = refs[0:4], refs[4:8], refs[8:10]
    acc, stats, kfar, vfar, kbuf, vbuf, qbuf, hides = refs[10:]
    x = x_ref[0]
    row = lax.broadcasted_iota(jnp.int32, (BLOCK, BLOCK), 0)
    col = lax.broadcasted_iota(jnp.int32, (BLOCK, BLOCK), 1)
    causal = col <= row
    empty = jnp.zeros((BLOCK, BLOCK), jnp.bfloat16)
    for d in range(RING):
        j = (x + RING - d) & 3
        hides[pl.ds(pl.multiple_of(j * 16, 16), 16), :] = qs[d][ROWS : ROWS + 16, 0:HEAD_DIM]

    for d in range(RING):
        j = (x + RING - d) & 3
        at = pl.ds(pl.multiple_of(j * ROWS, ROWS), ROWS)
        kbuf[at, :] = own[d][0:ROWS, :]
        spread_values(vbuf, at, own[d][ROWS : 2 * ROWS, :])
        qbuf[at, :] = qs[d][0:ROWS, :]

    def head(h):
        here = head_columns(h)
        for j in range(RING):
            width = (j + 1) * ROWS
            hide = hides[j * 16 : (j + 1) * 16, :].astype(jnp.float32)
            scores = dot_keys(qbuf[j * ROWS : (j + 1) * ROWS, here], kbuf[0:width, here])
            weights = []
            for r in range(2):
                a = 2 * j + r
                s = scores[r * BLOCK : (r + 1) * BLOCK, :]
                parts = []
                for g in range(a):
                    line = r * 8 + WINDOW - 1 - (a - g)
                    parts.append(s[:, g * BLOCK : (g + 1) * BLOCK] + hide[line : line + 1, :])
                parts.append(jnp.where(causal, s[:, a * BLOCK : (a + 1) * BLOCK], HIDE))
                top = jnp.max(fold(jnp.maximum, parts), axis=1, keepdims=True)
                parts = [jnp.exp2((part - top) * FACTOR) for part in parts]
                stats[a * BLOCK : (a + 1) * BLOCK, here] = jnp.broadcast_to(top, (BLOCK, BLOCK))
                parts = [part.astype(jnp.bfloat16) for part in parts]
                weights.append(jnp.concatenate(parts if r else parts + [empty], axis=1))
            p = jnp.concatenate(weights, axis=0)
            both = head_pair(h)
            acc[j * ROWS : (j + 1) * ROWS, both] = jnp.dot(
                p, vbuf[0:width, both], preferred_element_type=jnp.float32
            )

    heads_in_turn(head, NEAR_UNROLL)
    for d, piece, base in ((0, halo[0], 0), (1, halo[1], 0), (3, halo[1], 2 * ROWS)):
        place_halo(x, d, piece, base, kfar, vfar)


INSIDE = pl.BlockSpec(memory_space=pltpu.VMEM)
SCALARS = pl.BlockSpec(memory_space=pltpu.SMEM)
OUTSIDE = pl.BlockSpec(memory_space=pltpu.HBM)


def attend_near(x, own, qs, halo):
    return pl.pallas_call(
        near_kernel,
        out_shape=[
            jax.ShapeDtypeStruct((RING * ROWS, 2 * WIDTH), jnp.float32),
            jax.ShapeDtypeStruct((RING * ROWS, WIDTH), jnp.float32),
            jax.ShapeDtypeStruct((RING * ROWS, WIDTH), jnp.bfloat16),
            jax.ShapeDtypeStruct((RING * ROWS, 2 * WIDTH), jnp.bfloat16),
        ],
        in_specs=[SCALARS] + [INSIDE] * 10,
        out_specs=[INSIDE] * 4,
        scratch_shapes=[
            pltpu.VMEM((RING * ROWS, WIDTH), jnp.bfloat16),
            pltpu.VMEM((RING * ROWS, 2 * WIDTH), jnp.bfloat16),
            pltpu.VMEM((RING * ROWS, WIDTH), jnp.bfloat16),
            pltpu.VMEM((RING * 16, HEAD_DIM), jnp.bfloat16),
        ],
        compiler_params=pltpu.CompilerParams(vmem_limit_bytes=VMEM),
        cost_estimate=pl.CostEstimate(
            flops=1300000000, bytes_accessed=7000000, transcendentals=2400000
        ),
        name="attend_near",
    )(x, *own, *qs, *halo)


def far_kernel(order, fresh, x_ref, *refs):
    count = len(order)
    qs, refs = refs[0:count], refs[count:]
    acc, stats, kbuf, vbuf, refs = refs[0], refs[1], refs[2], refs[3], refs[4:]
    x = x_ref[0]
    if fresh:
        piece, outs, (kall, vall) = refs[0], refs[1 : 1 + count], refs[1 + count :]
        for d in (0, 1, 3):
            at = pl.ds(pl.multiple_of(((x + RING - d) & 3) * ROWS, ROWS), ROWS)
            kall[at, :] = kbuf[at, :]
            vall[at, :] = vbuf[at, :]
        kbuf, vbuf = kall, vall
        place_halo(x, 2, piece, 0, kbuf, vbuf)
    else:
        outs = refs

    def shard_piece(index, j, h):
        here = head_columns(h)
        begin = (2 * j + 1) * BLOCK
        blocks = WINDOW - 1 - 2 * j
        hide = qs[index][ROWS : ROWS + 16, 0:HEAD_DIM].astype(jnp.float32)
        scores = dot_keys(qs[index][0:ROWS, here], kbuf[begin : RING * ROWS, here])
        empty = jnp.zeros((BLOCK, BLOCK), jnp.bfloat16)
        state = stats[j * ROWS : (j + 1) * ROWS, here]
        weights, scales = [], []
        for r in range(2):
            rows = slice(r * BLOCK, (r + 1) * BLOCK)
            before = state[rows, :]
            s = scores[rows, :]
            parts = []
            for g in range(r, blocks):
                line = r * 8 + g - r
                parts.append(s[:, g * BLOCK : (g + 1) * BLOCK] + hide[line : line + 1, :])
            if not parts:
                weights.append(empty)
                scales.append(jnp.ones_like(before))
                continue
            top = jnp.max(fold(jnp.maximum, parts), axis=1, keepdims=True)
            top = jnp.maximum(before, top)
            scales.append(jnp.exp2((before - top) * FACTOR))
            parts = [jnp.exp2((part - top) * FACTOR).astype(jnp.bfloat16) for part in parts]
            weights.append(jnp.concatenate([empty] * r + parts, axis=1))
        p = jnp.concatenate(weights, axis=0)
        scale = jnp.concatenate(scales, axis=0)
        both = head_pair(h)
        o = jnp.dot(p, vbuf[begin : RING * ROWS, both], preferred_element_type=jnp.float32)
        o = o + acc[j * ROWS : (j + 1) * ROWS, both] * jnp.concatenate([scale, scale], axis=1)
        outs[index][:, here] = (o[:, 0:HEAD_DIM] / o[:, HEAD_DIM:]).astype(jnp.bfloat16)

    for index, d in enumerate(order):
        for j in range(RING):

            def heads(index=index, j=j):
                heads_in_turn(lambda h: shard_piece(index, j, h), FAR_UNROLL)

            pl.when(((x + RING - d) & 3) == j)(heads)


def attend_far(x, piece, qs, acc, stats, kfar, vfar, order):
    count = len(order)
    fresh = piece is not None
    buffers = [jax.ShapeDtypeStruct(a.shape, a.dtype) for a in (kfar, vfar)] if fresh else []
    result = pl.pallas_call(
        lambda *refs: far_kernel(order, fresh, *refs),
        out_shape=[jax.ShapeDtypeStruct((ROWS, WIDTH), jnp.bfloat16)] * count + buffers,
        in_specs=[SCALARS] + [INSIDE] * (4 + count + fresh),
        out_specs=[INSIDE] * (count + len(buffers)),
        compiler_params=pltpu.CompilerParams(vmem_limit_bytes=VMEM),
        cost_estimate=pl.CostEstimate(
            flops=count * 270000000, bytes_accessed=5000000, transcendentals=count * 500000
        ),
        name="attend_far",
    )(x, *[qs[d] for d in order], acc, stats, kfar, vfar, *([piece] if fresh else []))
    return (result[:count], *result[count:]) if fresh else result


TILE = 512


def project_first_kernel(keys, x_ref, *refs):
    count = len(keys)
    weight, out = refs[count:]
    x = x_ref[0]
    for n in range(D // TILE):
        columns = slice(n * TILE, (n + 1) * TILE)
        total = None
        for d, piece in zip(keys, refs[:count]):
            rows = column_block(x, d)
            term = jnp.dot(piece[...], weight[rows, columns], preferred_element_type=jnp.float32)
            total = term if total is None else total + term
        out[:, columns] = total


def project_last_kernel(keys, x_ref, *refs):
    count = len(keys)
    weight, before, hidden, send_ref, mine_ref = refs[count:]
    x, side = x_ref[0], x_ref[1]

    def product(half, n):
        columns = pl.ds(pl.multiple_of(half * HALF + n * TILE, TILE), TILE)
        total = before[:, columns]
        for d, piece in zip(keys, refs[:count]):
            rows = column_block(x, d)
            term = jnp.dot(piece[...], weight[rows, columns], preferred_element_type=jnp.float32)
            total = total + term
        return columns, total

    for n in range(HALF // TILE):
        columns, total = product(1 - side, n)
        send_ref[:, columns] = total.astype(jnp.bfloat16)
        here = slice(n * TILE, (n + 1) * TILE)
        columns, total = product(side, n)
        total = total + hidden[:, here].astype(jnp.float32)
        mine_ref[:, here] = total
        send_ref[:, columns] = total.astype(jnp.bfloat16)


def project_first(scalars, pieces, keys, weight):
    vmem = pl.BlockSpec(memory_space=pltpu.VMEM)
    return pl.pallas_call(
        lambda *refs: project_first_kernel(keys, *refs),
        out_shape=jax.ShapeDtypeStruct((ROWS, D), jnp.float32),
        in_specs=[pl.BlockSpec(memory_space=pltpu.SMEM)] + [vmem] * (len(keys) + 1),
        out_specs=vmem,
        compiler_params=pltpu.CompilerParams(vmem_limit_bytes=VMEM),
        cost_estimate=pl.CostEstimate(flops=3000000000, bytes_accessed=4000000, transcendentals=0),
        name="project_first",
    )(scalars, *[pieces[d] for d in keys], weight)


def project_last(scalars, pieces, keys, weight, before, hidden):
    vmem = pl.BlockSpec(memory_space=pltpu.VMEM)
    return pl.pallas_call(
        lambda *refs: project_last_kernel(keys, *refs),
        out_shape=[
            jax.ShapeDtypeStruct((ROWS, D), jnp.bfloat16),
            jax.ShapeDtypeStruct((ROWS, HALF), jnp.float32),
        ],
        in_specs=[pl.BlockSpec(memory_space=pltpu.SMEM)] + [vmem] * (3 + len(keys)),
        out_specs=[vmem] * 2,
        compiler_params=pltpu.CompilerParams(vmem_limit_bytes=VMEM),
        cost_estimate=pl.CostEstimate(flops=1000000000, bytes_accessed=4000000, transcendentals=0),
        name="project_last",
    )(scalars, *[pieces[d] for d in keys], weight, before, hidden)


STRIP = 16


def finish_kernel(s_ref, mine_ref, sent, came, gain, stream_out, normed_out, stream, normed, sems):
    side = pl.ds(pl.multiple_of(s_ref[1] * HALF, HALF), HALF)
    away = pl.ds(pl.multiple_of((1 - s_ref[1]) * HALF, HALF), HALF)
    copies = []
    for i in range(ROWS // STRIP):
        rows = pl.ds(i * STRIP, STRIP)
        mine = mine_ref[rows, :] + came[rows, side].astype(jnp.float32)
        rest = sent[rows, away].astype(jnp.float32) + came[rows, away].astype(jnp.float32)
        squares = jnp.sum(mine * mine + rest * rest, axis=1, keepdims=True)
        factor = lax.rsqrt(squares / D + 1e-06)
        stream[rows, :] = mine.astype(jnp.bfloat16)
        normed[rows, :] = (mine * factor * gain[...]).astype(jnp.bfloat16)
        for k, (a, b) in enumerate(((stream, stream_out), (normed, normed_out))):
            copy = pltpu.make_async_copy(a.at[rows, :], b.at[rows, :], sems.at[i, k])
            copy.start()
            copies.append(copy)
    for copy in copies:
        copy.wait()


def finish(scalars, mine, sent, came, gain):
    return pl.pallas_call(
        finish_kernel,
        out_shape=[jax.ShapeDtypeStruct((ROWS, HALF), jnp.bfloat16)] * 2,
        in_specs=[SCALARS] + [INSIDE] * 4,
        out_specs=[OUTSIDE] * 2,
        scratch_shapes=[pltpu.VMEM((ROWS, HALF), jnp.bfloat16)] * 2
        + [pltpu.SemaphoreType.DMA((ROWS // STRIP, 2))],
        compiler_params=pltpu.CompilerParams(vmem_limit_bytes=VMEM),
        cost_estimate=pl.CostEstimate(flops=10000000, bytes_accessed=8000000, transcendentals=256),
        name="finish",
    )(scalars, mine, sent, came, gain.reshape(1, HALF))


WHOLE_VMEM = 60 * 1024 * 1024


def column_block(x, d):
    return pl.ds(pl.multiple_of(((x + d) & 3) * WIDTH, WIDTH), WIDTH)


def run_copies(pairs, sems):
    copies = [pltpu.make_async_copy(a, b, sems.at[i]) for i, (a, b) in enumerate(pairs)]
    for copy in copies:
        copy.start()
    return copies


def pack_kv_kernel(order, scalars, keys, values, *refs):
    pairs = []
    for d, out in zip(order, refs):
        columns = column_block(scalars[0], d)
        pairs.append((keys.at[:, columns], out.at[pl.ds(0, ROWS), :]))
        pairs.append((values.at[:, columns], out.at[pl.ds(ROWS, ROWS), :]))
    for copy in run_copies(pairs, refs[-1]):
        copy.wait()


def pack_kv(scalars, keys, values, order):
    return pl.pallas_call(
        lambda *refs: pack_kv_kernel(order, *refs),
        out_shape=[jax.ShapeDtypeStruct((2 * ROWS, WIDTH), jnp.bfloat16)] * len(order),
        in_specs=[SCALARS] + [OUTSIDE] * 2,
        out_specs=[INSIDE] * len(order),
        scratch_shapes=[pltpu.SemaphoreType.DMA((2 * len(order),))],
        compiler_params=pltpu.CompilerParams(vmem_limit_bytes=WHOLE_VMEM),
        cost_estimate=pl.CostEstimate(flops=0, bytes_accessed=6000000, transcendentals=0),
        name="pack_kv",
    )(scalars, keys, values)


def pack_q_kernel(scalars, pattern, queries, *refs):
    qs, sems = refs[0:4], refs[4]
    first = scalars[2] * 2
    pairs = []
    for d in range(RING):
        pairs.append((queries.at[:, column_block(scalars[0], d)], qs[d].at[pl.ds(0, ROWS), :]))
    copies = run_copies(pairs, sems)
    row = lax.broadcasted_iota(jnp.int32, (16, WIDTH), 0)
    hide = jnp.zeros((16, WIDTH), jnp.float32)
    for r in range(2):
        for i in range(WINDOW - 1):
            back = WINDOW - 1 - i
            shown = (pattern[r, back] == 1) & (first + r - back >= 0)
            hide = jnp.where(row == r * 8 + i, jnp.where(shown, 0.0, HIDE), hide)
    for d in range(RING):
        qs[d][ROWS : ROWS + 16, :] = hide.astype(jnp.bfloat16)
    for copy in copies:
        copy.wait()


def pack_q(scalars, pattern, queries):
    return pl.pallas_call(
        pack_q_kernel,
        out_shape=[jax.ShapeDtypeStruct((ROWS + 16, WIDTH), jnp.bfloat16)] * 4,
        in_specs=[SCALARS, SCALARS, OUTSIDE],
        out_specs=[INSIDE] * 4,
        scratch_shapes=[pltpu.SemaphoreType.DMA((4,))],
        compiler_params=pltpu.CompilerParams(vmem_limit_bytes=WHOLE_VMEM),
        cost_estimate=pl.CostEstimate(flops=0, bytes_accessed=2000000, transcendentals=0),
        name="pack_q",
    )(scalars, pattern, queries)


def slice_kv(shard, keys, values, d):
    begin = ((shard + d) & 3) * WIDTH
    return jnp.concatenate(
        [lax.dynamic_slice(a, (jnp.int32(0), begin), (ROWS, WIDTH)) for a in (keys, values)], 0
    )


def shards(queries, key_rows, value_rows, block_pattern, out_weight, hidden, norm_gain):
    shard = lax.axis_index("seq").astype(jnp.int32)
    section = lax.axis_index("section").astype(jnp.int32)
    scalars = jnp.stack([shard & 3, section, shard])
    own, qs, halo = [None] * 4, [None] * 4, [None]
    right, left, own[0] = [slice_kv(shard, key_rows, value_rows, d) for d in (1, 3, 0)]
    later = after(scalars, right)
    (across,) = pack_kv(later, key_rows, value_rows, (2,))
    q = pack_q(later, block_pattern, queries)
    own[1] = ring_shift(right, 1)
    own[3] = ring_shift(left, 3)
    halo[0] = next_row(own[0])
    first = (own[1], own[3], halo[0])
    own[2] = ring_shift(after(across, *first, q[1], q[3]), 2)
    sides = next_row(after(jnp.concatenate([own[1], own[3]], 0), halo[0], across, q[1], q[3]))
    qs[0] = q[0]
    for d in (1, 3):
        qs[d] = ring_shift(after(q[d], *first), d)
    qs[2] = ring_shift(after(q[2], own[2]), 2)
    across = next_row(own[2])
    acc, stats, kfar, vfar = attend_near(scalars, own, qs, [halo[0], sides])
    pieces = {}
    (out,), kfar, vfar = attend_far(scalars, across, qs, acc, stats, kfar, vfar, (2,))
    pieces[2] = ring_shift(out, 2)
    (out,) = attend_far(scalars, None, qs, acc, stats, kfar, vfar, (1,))
    pieces[1] = ring_shift(out, 3)
    (out,) = attend_far(scalars, None, qs, acc, stats, kfar, vfar, (3,))
    pieces[3] = ring_shift(out, 1)
    (pieces[0],) = attend_far(scalars, None, qs, acc, stats, kfar, vfar, (0,))
    before = project_first(scalars, pieces, (0, 2), out_weight)
    sent, mine = project_last(scalars, pieces, (1, 3), out_weight, before, hidden)
    came = other_core(sent)
    return tuple(finish(scalars, mine, sent, came, norm_gain))


def solution(mesh):
    placed = (
        P("seq", "section"),
        P("seq", "section"),
        P("seq", "section"),
        P("seq", None),
        P("section", None),
        P("seq", "section"),
        P("section"),
    )
    return jax.shard_map(
        shards,
        mesh=mesh,
        in_specs=placed,
        out_specs=(P("seq", "section"), P("seq", "section")),
        check_vma=False,
    )
```

```python
import math

import jax
import jax.numpy as jnp
from jax import lax
from jax.experimental import pallas as pl
from jax.experimental.pallas import tpu as pltpu
from jax.sharding import PartitionSpec as P

D = 4096
HALF = 2048
HEAD_DIM = 128
BLOCK = 128
WINDOW = 8
ROWS = 256
RING = 4
WIDTH = 512
HIDE = -3e38
VMEM = 16 * 1024 * 1024


def ring_shift(array, d):
    route = [(i, (i // RING) * RING + (i + d) % RING) for i in range(128)]
    return lax.ppermute(array, "seq", route)


def next_row(array):
    return lax.ppermute(array, "seq", [(i, (i + RING) % 128) for i in range(128)])


def other_core(array):
    return lax.ppermute(array, "section", [(0, 1), (1, 0)])


def after(array, *others):
    return lax.optimization_barrier((array,) + others)[0]


FACTOR = math.log2(math.e) / math.sqrt(HEAD_DIM)


def dot_keys(q, keys):
    return lax.dot_general(q, keys, (((1,), (1,)), ((), ())), preferred_element_type=jnp.float32)


def fold(step, parts):
    result = parts[0]
    for part in parts[1:]:
        result = step(result, part)
    return result


NEAR_UNROLL = 4
FAR_UNROLL = 4


def heads_in_turn(head, unroll):
    def step(i, carry):
        for k in range(unroll):
            head(i * unroll + k)
        return carry

    if unroll == WIDTH // HEAD_DIM:
        step(0, 0)
    else:
        lax.fori_loop(0, WIDTH // HEAD_DIM // unroll, step, 0)


def head_columns(h):
    if isinstance(h, int):
        return slice(h * HEAD_DIM, (h + 1) * HEAD_DIM)
    return pl.ds(pl.multiple_of(h * HEAD_DIM, HEAD_DIM), HEAD_DIM)


def head_pair(h):
    if isinstance(h, int):
        return slice(h * 2 * HEAD_DIM, (h + 1) * 2 * HEAD_DIM)
    return pl.ds(pl.multiple_of(h * 2 * HEAD_DIM, 2 * HEAD_DIM), 2 * HEAD_DIM)


def spread_values(vbuf, at, values):
    ones = jnp.ones((ROWS, HEAD_DIM), jnp.bfloat16)
    for h in range(WIDTH // HEAD_DIM):
        here = slice(h * HEAD_DIM, (h + 1) * HEAD_DIM)
        vbuf[at, head_pair(h)] = jnp.concatenate([values[:, here], ones], axis=1)


def place_halo(x, d, keys, values, kfar, vfar):
    at = pl.ds(pl.multiple_of(((x + RING - d) & 3) * ROWS, ROWS), ROWS)
    kfar[at, :] = keys
    spread_values(vfar, at, values)


def near_kernel(x_ref, *refs):
    home, right_k, right_v, left_k, left_v, across = refs[0:6]
    qs, halo = refs[6:10], refs[10:13]
    acc, stats, kfar, vfar, kbuf, vbuf, qbuf, hides = refs[13:]
    own = (
        (home[0:ROWS, :], home[ROWS : 2 * ROWS, :]),
        (right_k[...], right_v[...]),
        (across[0:ROWS, :], across[ROWS : 2 * ROWS, :]),
        (left_k[...], left_v[...]),
    )
    x = x_ref[0]
    row = lax.broadcasted_iota(jnp.int32, (BLOCK, BLOCK), 0)
    col = lax.broadcasted_iota(jnp.int32, (BLOCK, BLOCK), 1)
    causal = col <= row
    empty = jnp.zeros((BLOCK, BLOCK), jnp.bfloat16)
    for d in range(RING):
        j = (x + RING - d) & 3
        hides[pl.ds(pl.multiple_of(j * 16, 16), 16), :] = qs[d][ROWS : ROWS + 16, 0:HEAD_DIM]

    for d in range(RING):
        j = (x + RING - d) & 3
        at = pl.ds(pl.multiple_of(j * ROWS, ROWS), ROWS)
        kbuf[at, :] = own[d][0]
        spread_values(vbuf, at, own[d][1])
        qbuf[at, :] = qs[d][0:ROWS, :]

    def head(h):
        here = head_columns(h)
        for j in range(RING):
            width = (j + 1) * ROWS
            hide = hides[j * 16 : (j + 1) * 16, :].astype(jnp.float32)
            scores = dot_keys(qbuf[j * ROWS : (j + 1) * ROWS, here], kbuf[0:width, here])
            weights = []
            for r in range(2):
                a = 2 * j + r
                s = scores[r * BLOCK : (r + 1) * BLOCK, :]
                parts = []
                for g in range(a):
                    line = r * 8 + WINDOW - 1 - (a - g)
                    parts.append(s[:, g * BLOCK : (g + 1) * BLOCK] + hide[line : line + 1, :])
                parts.append(jnp.where(causal, s[:, a * BLOCK : (a + 1) * BLOCK], HIDE))
                top = jnp.max(fold(jnp.maximum, parts), axis=1, keepdims=True)
                parts = [jnp.exp2((part - top) * FACTOR) for part in parts]
                stats[a * BLOCK : (a + 1) * BLOCK, here] = jnp.broadcast_to(top, (BLOCK, BLOCK))
                parts = [part.astype(jnp.bfloat16) for part in parts]
                weights.append(jnp.concatenate(parts if r else parts + [empty], axis=1))
            p = jnp.concatenate(weights, axis=0)
            both = head_pair(h)
            acc[j * ROWS : (j + 1) * ROWS, both] = jnp.dot(
                p, vbuf[0:width, both], preferred_element_type=jnp.float32
            )

    heads_in_turn(head, NEAR_UNROLL)
    home, side_k, side_v = halo
    place_halo(x, 0, home[0:ROWS, :], home[ROWS : 2 * ROWS, :], kfar, vfar)
    place_halo(x, 1, side_k[0:ROWS, :], side_v[0:ROWS, :], kfar, vfar)
    place_halo(x, 3, side_k[ROWS : 2 * ROWS, :], side_v[ROWS : 2 * ROWS, :], kfar, vfar)


INSIDE = pl.BlockSpec(memory_space=pltpu.VMEM)
SCALARS = pl.BlockSpec(memory_space=pltpu.SMEM)
OUTSIDE = pl.BlockSpec(memory_space=pltpu.HBM)


def attend_near(x, own, qs, halo):
    return pl.pallas_call(
        near_kernel,
        out_shape=[
            jax.ShapeDtypeStruct((RING * ROWS, 2 * WIDTH), jnp.float32),
            jax.ShapeDtypeStruct((RING * ROWS, WIDTH), jnp.float32),
            jax.ShapeDtypeStruct((RING * ROWS, WIDTH), jnp.bfloat16),
            jax.ShapeDtypeStruct((RING * ROWS, 2 * WIDTH), jnp.bfloat16),
        ],
        in_specs=[SCALARS] + [INSIDE] * 13,
        out_specs=[INSIDE] * 4,
        scratch_shapes=[
            pltpu.VMEM((RING * ROWS, WIDTH), jnp.bfloat16),
            pltpu.VMEM((RING * ROWS, 2 * WIDTH), jnp.bfloat16),
            pltpu.VMEM((RING * ROWS, WIDTH), jnp.bfloat16),
            pltpu.VMEM((RING * 16, HEAD_DIM), jnp.bfloat16),
        ],
        compiler_params=pltpu.CompilerParams(vmem_limit_bytes=VMEM),
        cost_estimate=pl.CostEstimate(
            flops=1300000000, bytes_accessed=7000000, transcendentals=2400000
        ),
        name="attend_near",
    )(x, *own, *qs, *halo)


def far_kernel(order, fresh, x_ref, *refs):
    count = len(order)
    qs, refs = refs[0:count], refs[count:]
    acc, stats, kbuf, vbuf, refs = refs[0], refs[1], refs[2], refs[3], refs[4:]
    x = x_ref[0]
    if fresh:
        piece, outs, (kall, vall) = refs[0], refs[1 : 1 + count], refs[1 + count :]
        for d in (0, 1, 3):
            at = pl.ds(pl.multiple_of(((x + RING - d) & 3) * ROWS, ROWS), ROWS)
            kall[at, :] = kbuf[at, :]
            vall[at, :] = vbuf[at, :]
        kbuf, vbuf = kall, vall
        place_halo(x, 2, piece[0:ROWS, :], piece[ROWS : 2 * ROWS, :], kbuf, vbuf)
    else:
        outs = refs

    def shard_piece(index, j, h):
        here = head_columns(h)
        begin = (2 * j + 1) * BLOCK
        blocks = WINDOW - 1 - 2 * j
        hide = qs[index][ROWS : ROWS + 16, 0:HEAD_DIM].astype(jnp.float32)
        scores = dot_keys(qs[index][0:ROWS, here], kbuf[begin : RING * ROWS, here])
        empty = jnp.zeros((BLOCK, BLOCK), jnp.bfloat16)
        state = stats[j * ROWS : (j + 1) * ROWS, here]
        weights, scales = [], []
        for r in range(2):
            rows = slice(r * BLOCK, (r + 1) * BLOCK)
            before = state[rows, :]
            s = scores[rows, :]
            parts = []
            for g in range(r, blocks):
                line = r * 8 + g - r
                parts.append(s[:, g * BLOCK : (g + 1) * BLOCK] + hide[line : line + 1, :])
            if not parts:
                weights.append(empty)
                scales.append(jnp.ones_like(before))
                continue
            top = jnp.max(fold(jnp.maximum, parts), axis=1, keepdims=True)
            top = jnp.maximum(before, top)
            scales.append(jnp.exp2((before - top) * FACTOR))
            parts = [jnp.exp2((part - top) * FACTOR).astype(jnp.bfloat16) for part in parts]
            weights.append(jnp.concatenate([empty] * r + parts, axis=1))
        p = jnp.concatenate(weights, axis=0)
        scale = jnp.concatenate(scales, axis=0)
        both = head_pair(h)
        o = jnp.dot(p, vbuf[begin : RING * ROWS, both], preferred_element_type=jnp.float32)
        o = o + acc[j * ROWS : (j + 1) * ROWS, both] * jnp.concatenate([scale, scale], axis=1)
        outs[index][:, here] = (o[:, 0:HEAD_DIM] / o[:, HEAD_DIM:]).astype(jnp.bfloat16)

    for index, d in enumerate(order):
        for j in range(RING):

            def heads(index=index, j=j):
                heads_in_turn(lambda h: shard_piece(index, j, h), FAR_UNROLL)

            pl.when(((x + RING - d) & 3) == j)(heads)


def attend_far(x, piece, qs, acc, stats, kfar, vfar, order):
    count = len(order)
    fresh = piece is not None
    buffers = [jax.ShapeDtypeStruct(a.shape, a.dtype) for a in (kfar, vfar)] if fresh else []
    result = pl.pallas_call(
        lambda *refs: far_kernel(order, fresh, *refs),
        out_shape=[jax.ShapeDtypeStruct((ROWS, WIDTH), jnp.bfloat16)] * count + buffers,
        in_specs=[SCALARS] + [INSIDE] * (4 + count + fresh),
        out_specs=[INSIDE] * (count + len(buffers)),
        compiler_params=pltpu.CompilerParams(vmem_limit_bytes=VMEM),
        cost_estimate=pl.CostEstimate(
            flops=count * 270000000, bytes_accessed=5000000, transcendentals=count * 500000
        ),
        name="attend_far",
    )(x, *[qs[d] for d in order], acc, stats, kfar, vfar, *([piece] if fresh else []))
    return (result[:count], *result[count:]) if fresh else result


TILE = 512


def project_first_kernel(keys, x_ref, *refs):
    count = len(keys)
    weight, out = refs[count:]
    x = x_ref[0]
    for n in range(D // TILE):
        columns = slice(n * TILE, (n + 1) * TILE)
        total = None
        for d, piece in zip(keys, refs[:count]):
            rows = column_block(x, d)
            term = jnp.dot(piece[...], weight[rows, columns], preferred_element_type=jnp.float32)
            total = term if total is None else total + term
        out[:, columns] = total


def project_last_kernel(keys, x_ref, *refs):
    count = len(keys)
    weight, before, hidden, send_ref, mine_ref = refs[count:]
    x, side = x_ref[0], x_ref[1]

    def product(half, n):
        columns = pl.ds(pl.multiple_of(half * HALF + n * TILE, TILE), TILE)
        total = before[:, columns]
        for d, piece in zip(keys, refs[:count]):
            rows = column_block(x, d)
            term = jnp.dot(piece[...], weight[rows, columns], preferred_element_type=jnp.float32)
            total = total + term
        return columns, total

    for n in range(HALF // TILE):
        columns, total = product(1 - side, n)
        send_ref[:, columns] = total.astype(jnp.bfloat16)
        here = slice(n * TILE, (n + 1) * TILE)
        columns, total = product(side, n)
        total = total + hidden[:, here].astype(jnp.float32)
        mine_ref[:, here] = total
        send_ref[:, columns] = total.astype(jnp.bfloat16)


def project_first(scalars, pieces, keys, weight):
    vmem = pl.BlockSpec(memory_space=pltpu.VMEM)
    return pl.pallas_call(
        lambda *refs: project_first_kernel(keys, *refs),
        out_shape=jax.ShapeDtypeStruct((ROWS, D), jnp.float32),
        in_specs=[pl.BlockSpec(memory_space=pltpu.SMEM)] + [vmem] * (len(keys) + 1),
        out_specs=vmem,
        compiler_params=pltpu.CompilerParams(vmem_limit_bytes=VMEM),
        cost_estimate=pl.CostEstimate(flops=3000000000, bytes_accessed=4000000, transcendentals=0),
        name="project_first",
    )(scalars, *[pieces[d] for d in keys], weight)


def project_last(scalars, pieces, keys, weight, before, hidden):
    vmem = pl.BlockSpec(memory_space=pltpu.VMEM)
    return pl.pallas_call(
        lambda *refs: project_last_kernel(keys, *refs),
        out_shape=[
            jax.ShapeDtypeStruct((ROWS, D), jnp.bfloat16),
            jax.ShapeDtypeStruct((ROWS, HALF), jnp.float32),
        ],
        in_specs=[pl.BlockSpec(memory_space=pltpu.SMEM)] + [vmem] * (3 + len(keys)),
        out_specs=[vmem] * 2,
        compiler_params=pltpu.CompilerParams(vmem_limit_bytes=VMEM),
        cost_estimate=pl.CostEstimate(flops=1000000000, bytes_accessed=4000000, transcendentals=0),
        name="project_last",
    )(scalars, *[pieces[d] for d in keys], weight, before, hidden)


STRIP = 16


def finish_kernel(s_ref, mine_ref, sent, came, gain, stream_out, normed_out, stream, normed, sems):
    side = pl.ds(pl.multiple_of(s_ref[1] * HALF, HALF), HALF)
    away = pl.ds(pl.multiple_of((1 - s_ref[1]) * HALF, HALF), HALF)
    copies = []
    for i in range(ROWS // STRIP):
        rows = pl.ds(i * STRIP, STRIP)
        mine = mine_ref[rows, :] + came[rows, side].astype(jnp.float32)
        rest = sent[rows, away].astype(jnp.float32) + came[rows, away].astype(jnp.float32)
        squares = jnp.sum(mine * mine + rest * rest, axis=1, keepdims=True)
        factor = lax.rsqrt(squares / D + 1e-06)
        stream[rows, :] = mine.astype(jnp.bfloat16)
        normed[rows, :] = (mine * factor * gain[...]).astype(jnp.bfloat16)
        for k, (a, b) in enumerate(((stream, stream_out), (normed, normed_out))):
            copy = pltpu.make_async_copy(a.at[rows, :], b.at[rows, :], sems.at[i, k])
            copy.start()
            copies.append(copy)
    for copy in copies:
        copy.wait()


def finish(scalars, mine, sent, came, gain):
    return pl.pallas_call(
        finish_kernel,
        out_shape=[jax.ShapeDtypeStruct((ROWS, HALF), jnp.bfloat16)] * 2,
        in_specs=[SCALARS] + [INSIDE] * 4,
        out_specs=[OUTSIDE] * 2,
        scratch_shapes=[pltpu.VMEM((ROWS, HALF), jnp.bfloat16)] * 2
        + [pltpu.SemaphoreType.DMA((ROWS // STRIP, 2))],
        compiler_params=pltpu.CompilerParams(vmem_limit_bytes=VMEM),
        cost_estimate=pl.CostEstimate(flops=10000000, bytes_accessed=8000000, transcendentals=256),
        name="finish",
    )(scalars, mine, sent, came, gain.reshape(1, HALF))


WHOLE_VMEM = 60 * 1024 * 1024


def column_block(x, d):
    return pl.ds(pl.multiple_of(((x + d) & 3) * WIDTH, WIDTH), WIDTH)


def run_copies(pairs, sems):
    copies = [pltpu.make_async_copy(a, b, sems.at[i]) for i, (a, b) in enumerate(pairs)]
    for copy in copies:
        copy.start()
    return copies


def pack_kv_kernel(order, scalars, keys, values, *refs):
    pairs = []
    for d, out in zip(order, refs):
        columns = column_block(scalars[0], d)
        pairs.append((keys.at[:, columns], out.at[pl.ds(0, ROWS), :]))
        pairs.append((values.at[:, columns], out.at[pl.ds(ROWS, ROWS), :]))
    for copy in run_copies(pairs, refs[-1]):
        copy.wait()


def pack_kv(scalars, keys, values, order):
    return pl.pallas_call(
        lambda *refs: pack_kv_kernel(order, *refs),
        out_shape=[jax.ShapeDtypeStruct((2 * ROWS, WIDTH), jnp.bfloat16)] * len(order),
        in_specs=[SCALARS] + [OUTSIDE] * 2,
        out_specs=[INSIDE] * len(order),
        scratch_shapes=[pltpu.SemaphoreType.DMA((2 * len(order),))],
        compiler_params=pltpu.CompilerParams(vmem_limit_bytes=WHOLE_VMEM),
        cost_estimate=pl.CostEstimate(flops=0, bytes_accessed=6000000, transcendentals=0),
        name="pack_kv",
    )(scalars, keys, values)


def pack_q_kernel(scalars, pattern, queries, *refs):
    qs, sems = refs[0:4], refs[4]
    first = scalars[2] * 2
    pairs = []
    for d in range(RING):
        pairs.append((queries.at[:, column_block(scalars[0], d)], qs[d].at[pl.ds(0, ROWS), :]))
    copies = run_copies(pairs, sems)
    row = lax.broadcasted_iota(jnp.int32, (16, WIDTH), 0)
    hide = jnp.zeros((16, WIDTH), jnp.float32)
    for r in range(2):
        for i in range(WINDOW - 1):
            back = WINDOW - 1 - i
            shown = (pattern[r, back] == 1) & (first + r - back >= 0)
            hide = jnp.where(row == r * 8 + i, jnp.where(shown, 0.0, HIDE), hide)
    for d in range(RING):
        qs[d][ROWS : ROWS + 16, :] = hide.astype(jnp.bfloat16)
    for copy in copies:
        copy.wait()


def pack_q(scalars, pattern, queries):
    return pl.pallas_call(
        pack_q_kernel,
        out_shape=[jax.ShapeDtypeStruct((ROWS + 16, WIDTH), jnp.bfloat16)] * 4,
        in_specs=[SCALARS, SCALARS, OUTSIDE],
        out_specs=[INSIDE] * 4,
        scratch_shapes=[pltpu.SemaphoreType.DMA((4,))],
        compiler_params=pltpu.CompilerParams(vmem_limit_bytes=WHOLE_VMEM),
        cost_estimate=pl.CostEstimate(flops=0, bytes_accessed=2000000, transcendentals=0),
        name="pack_q",
    )(scalars, pattern, queries)


def take_columns(shard, array, d):
    begin = ((shard + d) & 3) * WIDTH
    return lax.dynamic_slice(array, (jnp.int32(0), begin), (ROWS, WIDTH))


def shards(queries, key_rows, value_rows, block_pattern, out_weight, hidden, norm_gain):
    shard = lax.axis_index("seq").astype(jnp.int32)
    section = lax.axis_index("section").astype(jnp.int32)
    scalars = jnp.stack([shard & 3, section, shard])
    keys = {d: take_columns(shard, key_rows, d) for d in (1, 3, 0)}
    values = {d: take_columns(shard, value_rows, d) for d in (1, 3, 0)}
    home = jnp.concatenate([keys[0], values[0]], 0)
    later = after(scalars, keys[1])
    (across,) = pack_kv(later, key_rows, value_rows, (2,))
    q = pack_q(later, block_pattern, queries)
    near_k = {d: ring_shift(keys[d], d) for d in (1, 3)}
    home_halo = next_row(home)
    ready = (near_k[1], near_k[3], across, q[1])
    near_v = {d: ring_shift(after(values[d], *ready), d) for d in (1, 3)}
    across = ring_shift(after(across, *ready), 2)
    side_k = next_row(after(jnp.concatenate([near_k[1], near_k[3]], 0), q[1]))
    side_v = next_row(jnp.concatenate([near_v[1], near_v[3]], 0))
    qs = [q[0], None, None, None]
    for d in (1, 3):
        qs[d] = ring_shift(after(q[d], near_v[1], near_v[3]), d)
    qs[2] = ring_shift(after(q[2], across), 2)
    own = (home, near_k[1], near_v[1], near_k[3], near_v[3], across)
    across = next_row(across)
    acc, stats, kfar, vfar = attend_near(scalars, own, qs, (home_halo, side_k, side_v))
    pieces = {}
    (out,), kfar, vfar = attend_far(scalars, across, qs, acc, stats, kfar, vfar, (2,))
    pieces[2] = ring_shift(out, 2)
    (out,) = attend_far(scalars, None, qs, acc, stats, kfar, vfar, (1,))
    pieces[1] = ring_shift(out, 3)
    (out,) = attend_far(scalars, None, qs, acc, stats, kfar, vfar, (3,))
    pieces[3] = ring_shift(out, 1)
    (pieces[0],) = attend_far(scalars, None, qs, acc, stats, kfar, vfar, (0,))
    before = project_first(scalars, pieces, (0, 2), out_weight)
    sent, mine = project_last(scalars, pieces, (1, 3), out_weight, before, hidden)
    came = other_core(sent)
    return tuple(finish(scalars, mine, sent, came, norm_gain))


def solution(mesh):
    placed = (
        P("seq", "section"),
        P("seq", "section"),
        P("seq", "section"),
        P("seq", None),
        P("section", None),
        P("seq", "section"),
        P("section"),
    )
    return jax.shard_map(
        shards,
        mesh=mesh,
        in_specs=placed,
        out_specs=(P("seq", "section"), P("seq", "section")),
        check_vma=False,
    )
```

```python
import math

import jax
import jax.numpy as jnp
from jax import lax
from jax.experimental import pallas as pl
from jax.experimental.pallas import tpu as pltpu
from jax.sharding import PartitionSpec as P

D = 4096
HALF = 2048
HEAD_DIM = 128
BLOCK = 128
WINDOW = 8
ROWS = 256
RING = 4
WIDTH = 512
HIDE = -3e38
VMEM = 16 * 1024 * 1024


def ring_shift(array, d):
    route = [(i, (i // RING) * RING + (i + d) % RING) for i in range(128)]
    return lax.ppermute(array, "seq", route)


def next_row(array):
    return lax.ppermute(array, "seq", [(i, (i + RING) % 128) for i in range(128)])


def other_core(array):
    return lax.ppermute(array, "section", [(0, 1), (1, 0)])


def after(array, *others):
    return lax.optimization_barrier((array,) + others)[0]


FACTOR = math.log2(math.e) / math.sqrt(HEAD_DIM)


def dot_keys(q, keys):
    return lax.dot_general(q, keys, (((1,), (1,)), ((), ())), preferred_element_type=jnp.float32)


def fold(step, parts):
    result = parts[0]
    for part in parts[1:]:
        result = step(result, part)
    return result


NEAR_UNROLL = 4
FAR_UNROLL = 2


def heads_in_turn(head, unroll):
    def step(i, carry):
        for k in range(unroll):
            head(i * unroll + k)
        return carry

    if unroll == WIDTH // HEAD_DIM:
        step(0, 0)
    else:
        lax.fori_loop(0, WIDTH // HEAD_DIM // unroll, step, 0)


def head_columns(h):
    if isinstance(h, int):
        return slice(h * HEAD_DIM, (h + 1) * HEAD_DIM)
    return pl.ds(pl.multiple_of(h * HEAD_DIM, HEAD_DIM), HEAD_DIM)


def head_pair(h):
    if isinstance(h, int):
        return slice(h * 2 * HEAD_DIM, (h + 1) * 2 * HEAD_DIM)
    return pl.ds(pl.multiple_of(h * 2 * HEAD_DIM, 2 * HEAD_DIM), 2 * HEAD_DIM)


def spread_values(vbuf, at, values):
    ones = jnp.ones((ROWS, HEAD_DIM), jnp.bfloat16)
    for h in range(WIDTH // HEAD_DIM):
        here = slice(h * HEAD_DIM, (h + 1) * HEAD_DIM)
        vbuf[at, head_pair(h)] = jnp.concatenate([values[:, here], ones], axis=1)


def place_halo(x, d, keys, values, kfar, vfar):
    at = pl.ds(pl.multiple_of(((x + RING - d) & 3) * ROWS, ROWS), ROWS)
    kfar[at, :] = keys
    spread_values(vfar, at, values)


def near_kernel(x_ref, *refs):
    home, right_k, right_v, left_k, left_v, across = refs[0:6]
    qs, halo = refs[6:10], refs[10:13]
    acc, stats, kfar, vfar, kbuf, vbuf, qbuf, hides = refs[13:]
    own = (
        (home[0:ROWS, :], home[ROWS : 2 * ROWS, :]),
        (right_k[...], right_v[...]),
        (across[0:ROWS, :], across[ROWS : 2 * ROWS, :]),
        (left_k[...], left_v[...]),
    )
    x = x_ref[0]
    row = lax.broadcasted_iota(jnp.int32, (BLOCK, BLOCK), 0)
    col = lax.broadcasted_iota(jnp.int32, (BLOCK, BLOCK), 1)
    causal = col <= row
    empty = jnp.zeros((BLOCK, BLOCK), jnp.bfloat16)
    for d in range(RING):
        j = (x + RING - d) & 3
        hides[pl.ds(pl.multiple_of(j * 16, 16), 16), :] = qs[d][ROWS : ROWS + 16, 0:HEAD_DIM]

    for d in range(RING):
        j = (x + RING - d) & 3
        at = pl.ds(pl.multiple_of(j * ROWS, ROWS), ROWS)
        kbuf[at, :] = own[d][0]
        spread_values(vbuf, at, own[d][1])
        qbuf[at, :] = qs[d][0:ROWS, :]

    def head(h):
        here = head_columns(h)
        for j in range(RING):
            width = (j + 1) * ROWS
            hide = hides[j * 16 : (j + 1) * 16, :].astype(jnp.float32)
            scores = dot_keys(qbuf[j * ROWS : (j + 1) * ROWS, here], kbuf[0:width, here])
            weights = []
            for r in range(2):
                a = 2 * j + r
                s = scores[r * BLOCK : (r + 1) * BLOCK, :]
                parts = []
                for g in range(a):
                    line = r * 8 + WINDOW - 1 - (a - g)
                    parts.append(s[:, g * BLOCK : (g + 1) * BLOCK] + hide[line : line + 1, :])
                parts.append(jnp.where(causal, s[:, a * BLOCK : (a + 1) * BLOCK], HIDE))
                top = jnp.max(fold(jnp.maximum, parts), axis=1, keepdims=True)
                parts = [jnp.exp2((part - top) * FACTOR) for part in parts]
                stats[a * BLOCK : (a + 1) * BLOCK, here] = jnp.broadcast_to(top, (BLOCK, BLOCK))
                parts = [part.astype(jnp.bfloat16) for part in parts]
                weights.append(jnp.concatenate(parts if r else parts + [empty], axis=1))
            p = jnp.concatenate(weights, axis=0)
            both = head_pair(h)
            acc[j * ROWS : (j + 1) * ROWS, both] = jnp.dot(
                p, vbuf[0:width, both], preferred_element_type=jnp.float32
            )

    heads_in_turn(head, NEAR_UNROLL)
    home, side_k, side_v = halo
    place_halo(x, 0, home[0:ROWS, :], home[ROWS : 2 * ROWS, :], kfar, vfar)
    place_halo(x, 1, side_k[0:ROWS, :], side_v[0:ROWS, :], kfar, vfar)
    place_halo(x, 3, side_k[ROWS : 2 * ROWS, :], side_v[ROWS : 2 * ROWS, :], kfar, vfar)


INSIDE = pl.BlockSpec(memory_space=pltpu.VMEM)
SCALARS = pl.BlockSpec(memory_space=pltpu.SMEM)
OUTSIDE = pl.BlockSpec(memory_space=pltpu.HBM)


def attend_near(x, own, qs, halo):
    return pl.pallas_call(
        near_kernel,
        out_shape=[
            jax.ShapeDtypeStruct((RING * ROWS, 2 * WIDTH), jnp.float32),
            jax.ShapeDtypeStruct((RING * ROWS, WIDTH), jnp.float32),
            jax.ShapeDtypeStruct((RING * ROWS, WIDTH), jnp.bfloat16),
            jax.ShapeDtypeStruct((RING * ROWS, 2 * WIDTH), jnp.bfloat16),
        ],
        in_specs=[SCALARS] + [INSIDE] * 13,
        out_specs=[INSIDE] * 4,
        scratch_shapes=[
            pltpu.VMEM((RING * ROWS, WIDTH), jnp.bfloat16),
            pltpu.VMEM((RING * ROWS, 2 * WIDTH), jnp.bfloat16),
            pltpu.VMEM((RING * ROWS, WIDTH), jnp.bfloat16),
            pltpu.VMEM((RING * 16, HEAD_DIM), jnp.bfloat16),
        ],
        compiler_params=pltpu.CompilerParams(vmem_limit_bytes=VMEM),
        cost_estimate=pl.CostEstimate(
            flops=1300000000, bytes_accessed=7000000, transcendentals=2400000
        ),
        name="attend_near",
    )(x, *own, *qs, *halo)


def far_kernel(order, fresh, x_ref, *refs):
    count = len(order)
    qs, refs = refs[0:count], refs[count:]
    acc, stats, kbuf, vbuf, refs = refs[0], refs[1], refs[2], refs[3], refs[4:]
    x = x_ref[0]
    if fresh:
        piece, outs, (kall, vall) = refs[0], refs[1 : 1 + count], refs[1 + count :]
        for d in (0, 1, 3):
            at = pl.ds(pl.multiple_of(((x + RING - d) & 3) * ROWS, ROWS), ROWS)
            kall[at, :] = kbuf[at, :]
            vall[at, :] = vbuf[at, :]
        kbuf, vbuf = kall, vall
        place_halo(x, 2, piece[0:ROWS, :], piece[ROWS : 2 * ROWS, :], kbuf, vbuf)
    else:
        outs = refs

    def shard_piece(index, j, h):
        here = head_columns(h)
        begin = (2 * j + 1) * BLOCK
        blocks = WINDOW - 1 - 2 * j
        hide = qs[index][ROWS : ROWS + 16, 0:HEAD_DIM].astype(jnp.float32)
        scores = dot_keys(qs[index][0:ROWS, here], kbuf[begin : RING * ROWS, here])
        empty = jnp.zeros((BLOCK, BLOCK), jnp.bfloat16)
        state = stats[j * ROWS : (j + 1) * ROWS, here]
        weights, scales = [], []
        for r in range(2):
            rows = slice(r * BLOCK, (r + 1) * BLOCK)
            before = state[rows, :]
            s = scores[rows, :]
            parts = []
            for g in range(r, blocks):
                line = r * 8 + g - r
                parts.append(s[:, g * BLOCK : (g + 1) * BLOCK] + hide[line : line + 1, :])
            if not parts:
                weights.append(empty)
                scales.append(jnp.ones_like(before))
                continue
            top = jnp.max(fold(jnp.maximum, parts), axis=1, keepdims=True)
            top = jnp.maximum(before, top)
            scales.append(jnp.exp2((before - top) * FACTOR))
            parts = [jnp.exp2((part - top) * FACTOR).astype(jnp.bfloat16) for part in parts]
            weights.append(jnp.concatenate([empty] * r + parts, axis=1))
        p = jnp.concatenate(weights, axis=0)
        scale = jnp.concatenate(scales, axis=0)
        both = head_pair(h)
        o = jnp.dot(p, vbuf[begin : RING * ROWS, both], preferred_element_type=jnp.float32)
        o = o + acc[j * ROWS : (j + 1) * ROWS, both] * jnp.concatenate([scale, scale], axis=1)
        outs[index][:, here] = (o[:, 0:HEAD_DIM] / o[:, HEAD_DIM:]).astype(jnp.bfloat16)

    for index, d in enumerate(order):
        for j in range(RING):

            def heads(index=index, j=j):
                heads_in_turn(lambda h: shard_piece(index, j, h), FAR_UNROLL)

            pl.when(((x + RING - d) & 3) == j)(heads)


def attend_far(x, piece, qs, acc, stats, kfar, vfar, order):
    count = len(order)
    fresh = piece is not None
    buffers = [jax.ShapeDtypeStruct(a.shape, a.dtype) for a in (kfar, vfar)] if fresh else []
    result = pl.pallas_call(
        lambda *refs: far_kernel(order, fresh, *refs),
        out_shape=[jax.ShapeDtypeStruct((ROWS, WIDTH), jnp.bfloat16)] * count + buffers,
        in_specs=[SCALARS] + [INSIDE] * (4 + count + fresh),
        out_specs=[INSIDE] * (count + len(buffers)),
        compiler_params=pltpu.CompilerParams(vmem_limit_bytes=VMEM),
        cost_estimate=pl.CostEstimate(
            flops=count * 270000000, bytes_accessed=5000000, transcendentals=count * 500000
        ),
        name="attend_far",
    )(x, *[qs[d] for d in order], acc, stats, kfar, vfar, *([piece] if fresh else []))
    return (result[:count], *result[count:]) if fresh else result


TILE = 512


def project_first_kernel(keys, x_ref, *refs):
    count = len(keys)
    weight, out = refs[count:]
    x = x_ref[0]
    for n in range(D // TILE):
        columns = slice(n * TILE, (n + 1) * TILE)
        total = None
        for d, piece in zip(keys, refs[:count]):
            rows = column_block(x, d)
            term = jnp.dot(piece[...], weight[rows, columns], preferred_element_type=jnp.float32)
            total = term if total is None else total + term
        out[:, columns] = total


def project_last_kernel(keys, x_ref, *refs):
    count = len(keys)
    weight, before, hidden, send_ref, mine_ref = refs[count:]
    x, side = x_ref[0], x_ref[1]

    def product(half, n):
        columns = pl.ds(pl.multiple_of(half * HALF + n * TILE, TILE), TILE)
        total = before[:, columns]
        for d, piece in zip(keys, refs[:count]):
            rows = column_block(x, d)
            term = jnp.dot(piece[...], weight[rows, columns], preferred_element_type=jnp.float32)
            total = total + term
        return columns, total

    for n in range(HALF // TILE):
        columns, total = product(1 - side, n)
        send_ref[:, columns] = total.astype(jnp.bfloat16)
        here = slice(n * TILE, (n + 1) * TILE)
        columns, total = product(side, n)
        total = total + hidden[:, here].astype(jnp.float32)
        mine_ref[:, here] = total
        send_ref[:, columns] = total.astype(jnp.bfloat16)


def project_first(scalars, pieces, keys, weight):
    vmem = pl.BlockSpec(memory_space=pltpu.VMEM)
    return pl.pallas_call(
        lambda *refs: project_first_kernel(keys, *refs),
        out_shape=jax.ShapeDtypeStruct((ROWS, D), jnp.float32),
        in_specs=[pl.BlockSpec(memory_space=pltpu.SMEM)] + [vmem] * (len(keys) + 1),
        out_specs=vmem,
        compiler_params=pltpu.CompilerParams(vmem_limit_bytes=VMEM),
        cost_estimate=pl.CostEstimate(flops=3000000000, bytes_accessed=4000000, transcendentals=0),
        name="project_first",
    )(scalars, *[pieces[d] for d in keys], weight)


def project_last(scalars, pieces, keys, weight, before, hidden):
    vmem = pl.BlockSpec(memory_space=pltpu.VMEM)
    return pl.pallas_call(
        lambda *refs: project_last_kernel(keys, *refs),
        out_shape=[
            jax.ShapeDtypeStruct((ROWS, D), jnp.bfloat16),
            jax.ShapeDtypeStruct((ROWS, HALF), jnp.float32),
        ],
        in_specs=[pl.BlockSpec(memory_space=pltpu.SMEM)] + [vmem] * (3 + len(keys)),
        out_specs=[vmem] * 2,
        compiler_params=pltpu.CompilerParams(vmem_limit_bytes=VMEM),
        cost_estimate=pl.CostEstimate(flops=1000000000, bytes_accessed=4000000, transcendentals=0),
        name="project_last",
    )(scalars, *[pieces[d] for d in keys], weight, before, hidden)


STRIP = 16


def finish_kernel(s_ref, mine_ref, sent, came, gain, stream_out, normed_out, stream, normed, sems):
    side = pl.ds(pl.multiple_of(s_ref[1] * HALF, HALF), HALF)
    away = pl.ds(pl.multiple_of((1 - s_ref[1]) * HALF, HALF), HALF)
    copies = []
    for i in range(ROWS // STRIP):
        rows = pl.ds(i * STRIP, STRIP)
        mine = mine_ref[rows, :] + came[rows, side].astype(jnp.float32)
        rest = sent[rows, away].astype(jnp.float32) + came[rows, away].astype(jnp.float32)
        squares = jnp.sum(mine * mine + rest * rest, axis=1, keepdims=True)
        factor = lax.rsqrt(squares / D + 1e-06)
        stream[rows, :] = mine.astype(jnp.bfloat16)
        normed[rows, :] = (mine * factor * gain[...]).astype(jnp.bfloat16)
        for k, (a, b) in enumerate(((stream, stream_out), (normed, normed_out))):
            copy = pltpu.make_async_copy(a.at[rows, :], b.at[rows, :], sems.at[i, k])
            copy.start()
            copies.append(copy)
    for copy in copies:
        copy.wait()


def finish(scalars, mine, sent, came, gain):
    return pl.pallas_call(
        finish_kernel,
        out_shape=[jax.ShapeDtypeStruct((ROWS, HALF), jnp.bfloat16)] * 2,
        in_specs=[SCALARS] + [INSIDE] * 4,
        out_specs=[OUTSIDE] * 2,
        scratch_shapes=[pltpu.VMEM((ROWS, HALF), jnp.bfloat16)] * 2
        + [pltpu.SemaphoreType.DMA((ROWS // STRIP, 2))],
        compiler_params=pltpu.CompilerParams(vmem_limit_bytes=VMEM),
        cost_estimate=pl.CostEstimate(flops=10000000, bytes_accessed=8000000, transcendentals=256),
        name="finish",
    )(scalars, mine, sent, came, gain.reshape(1, HALF))


WHOLE_VMEM = 60 * 1024 * 1024


def column_block(x, d):
    return pl.ds(pl.multiple_of(((x + d) & 3) * WIDTH, WIDTH), WIDTH)


def run_copies(pairs, sems):
    copies = [pltpu.make_async_copy(a, b, sems.at[i]) for i, (a, b) in enumerate(pairs)]
    for copy in copies:
        copy.start()
    return copies


def pack_kv_kernel(order, scalars, keys, values, *refs):
    pairs = []
    for d, out in zip(order, refs):
        columns = column_block(scalars[0], d)
        pairs.append((keys.at[:, columns], out.at[pl.ds(0, ROWS), :]))
        pairs.append((values.at[:, columns], out.at[pl.ds(ROWS, ROWS), :]))
    for copy in run_copies(pairs, refs[-1]):
        copy.wait()


def pack_kv(scalars, keys, values, order):
    return pl.pallas_call(
        lambda *refs: pack_kv_kernel(order, *refs),
        out_shape=[jax.ShapeDtypeStruct((2 * ROWS, WIDTH), jnp.bfloat16)] * len(order),
        in_specs=[SCALARS] + [OUTSIDE] * 2,
        out_specs=[INSIDE] * len(order),
        scratch_shapes=[pltpu.SemaphoreType.DMA((2 * len(order),))],
        compiler_params=pltpu.CompilerParams(vmem_limit_bytes=WHOLE_VMEM),
        cost_estimate=pl.CostEstimate(flops=0, bytes_accessed=6000000, transcendentals=0),
        name="pack_kv",
    )(scalars, keys, values)


def pack_q_kernel(scalars, pattern, queries, *refs):
    qs, sems = refs[0:4], refs[4]
    first = scalars[2] * 2
    pairs = []
    for d in range(RING):
        pairs.append((queries.at[:, column_block(scalars[0], d)], qs[d].at[pl.ds(0, ROWS), :]))
    copies = run_copies(pairs, sems)
    row = lax.broadcasted_iota(jnp.int32, (16, WIDTH), 0)
    hide = jnp.zeros((16, WIDTH), jnp.float32)
    for r in range(2):
        for i in range(WINDOW - 1):
            back = WINDOW - 1 - i
            shown = (pattern[r, back] == 1) & (first + r - back >= 0)
            hide = jnp.where(row == r * 8 + i, jnp.where(shown, 0.0, HIDE), hide)
    for d in range(RING):
        qs[d][ROWS : ROWS + 16, :] = hide.astype(jnp.bfloat16)
    for copy in copies:
        copy.wait()


def pack_q(scalars, pattern, queries):
    return pl.pallas_call(
        pack_q_kernel,
        out_shape=[jax.ShapeDtypeStruct((ROWS + 16, WIDTH), jnp.bfloat16)] * 4,
        in_specs=[SCALARS, SCALARS, OUTSIDE],
        out_specs=[INSIDE] * 4,
        scratch_shapes=[pltpu.SemaphoreType.DMA((4,))],
        compiler_params=pltpu.CompilerParams(vmem_limit_bytes=WHOLE_VMEM),
        cost_estimate=pl.CostEstimate(flops=0, bytes_accessed=2000000, transcendentals=0),
        name="pack_q",
    )(scalars, pattern, queries)


def take_columns(shard, array, d):
    begin = ((shard + d) & 3) * WIDTH
    return lax.dynamic_slice(array, (jnp.int32(0), begin), (ROWS, WIDTH))


def shards(queries, key_rows, value_rows, block_pattern, out_weight, hidden, norm_gain):
    shard = lax.axis_index("seq").astype(jnp.int32)
    section = lax.axis_index("section").astype(jnp.int32)
    scalars = jnp.stack([shard & 3, section, shard])
    keys = {d: take_columns(shard, key_rows, d) for d in (1, 3, 0)}
    values = {d: take_columns(shard, value_rows, d) for d in (1, 3, 0)}
    home = jnp.concatenate([keys[0], values[0]], 0)
    later = after(scalars, keys[1])
    (across,) = pack_kv(later, key_rows, value_rows, (2,))
    q = pack_q(later, block_pattern, queries)
    near_k = {d: ring_shift(keys[d], d) for d in (1, 3)}
    home_halo = next_row(home)
    ready = (near_k[1], near_k[3], across, q[1])
    near_v = {d: ring_shift(after(values[d], *ready), d) for d in (1, 3)}
    across = ring_shift(after(across, *ready), 2)
    side_k = next_row(after(jnp.concatenate([near_k[1], near_k[3]], 0), q[1]))
    side_v = next_row(jnp.concatenate([near_v[1], near_v[3]], 0))
    qs = [q[0], None, None, None]
    for d in (1, 3):
        qs[d] = ring_shift(after(q[d], near_v[1], near_v[3]), d)
    qs[2] = ring_shift(after(q[2], across), 2)
    own = (home, near_k[1], near_v[1], near_k[3], near_v[3], across)
    across = next_row(across)
    acc, stats, kfar, vfar = attend_near(scalars, own, qs, (home_halo, side_k, side_v))
    pieces = {}
    (out,), kfar, vfar = attend_far(scalars, across, qs, acc, stats, kfar, vfar, (2,))
    pieces[2] = ring_shift(out, 2)
    (out,) = attend_far(scalars, None, qs, acc, stats, kfar, vfar, (1,))
    pieces[1] = ring_shift(out, 3)
    (out,) = attend_far(scalars, None, qs, acc, stats, kfar, vfar, (3,))
    pieces[3] = ring_shift(out, 1)
    (pieces[0],) = attend_far(scalars, None, qs, acc, stats, kfar, vfar, (0,))
    before = project_first(scalars, pieces, (0, 2), out_weight)
    sent, mine = project_last(scalars, pieces, (1, 3), out_weight, before, hidden)
    came = other_core(sent)
    return tuple(finish(scalars, mine, sent, came, norm_gain))


def solution(mesh):
    placed = (
        P("seq", "section"),
        P("seq", "section"),
        P("seq", "section"),
        P("seq", None),
        P("section", None),
        P("seq", "section"),
        P("section"),
    )
    return jax.shard_map(
        shards,
        mesh=mesh,
        in_specs=placed,
        out_specs=(P("seq", "section"), P("seq", "section")),
        check_vma=False,
    )
```
